512 devices in a mesh: row: 64 (over x_lo, z, core), col: 8 (over x_hi, y).
Axes of the slice: x: 4 (x_hi: 2, x_lo: 2; x = x_hi * 2 + x_lo), y: 4, z: 16, core: 2. Of those that a mesh axis runs over, the one named last changes fastest.
Arguments:
- amplitudes: bfloat16 [1024, 160000], P(('row', 'col')), may hold values from -6 to 6
- integrals: bfloat16 [160000, 1024], P('row', 'col'), may hold values from -0.03125 to 0.03125
- occ_irreps: int32 [50], replicated, may hold values from 0 to 3
- block_sizes: int32 [4], replicated, may hold values from 1 to 160, 400 in all
Outputs:
- ladder: bfloat16 [1024, 1024], P('row', 'col')
The draws below stay inside these ranges and needn't reach their ends.
Inputs may be any that keep to these rules, and one draw needn't show every extreme that they name: `block_sizes`: the virtual orbitals are ordered by irrep; these are the sizes of the 4 blocks, summing to 400.
All inputs are finite; a program needn't handle non-finite values.
Results may differ from the reference program's by a relative error of at most 0.003.
Values may be sent and summed in bfloat16 or wider, within the bound.
No kernel may reach another device: no remote copies, remote signals or barrier semaphores. Data moves between devices by JAX's collectives and lax.ppermute only.
A program may use at most 64 MiB of HBM per device.

```python
import math
import jax
import jax.numpy as jnp
import numpy as np
from jax import lax

OCCUPIED = 50
VIRTUAL = 400
IRREPS = 4
OCC_PAIRS = 1024
VIRT_PAIRS = 160000
OUT_PAIRS = 1024


def touch_ends(drawn, own_key, least, top_value):
    longest = drawn.shape.index(max(drawn.shape))
    spots = []
    for shift in (0, 1):
        where = [jax.random.randint(jax.random.fold_in(own_key, axis), (), 0, length) for axis, length in enumerate(drawn.shape)]
        where[longest] = (where[longest] + shift) % drawn.shape[longest]
        spots.append(tuple(where))
    return drawn.at[spots[0]].set(least).at[spots[1]].set(top_value)


def block_scale(stream_key, extent, shards, smallest, top_value):
    loudness = 1.0
    for dim, shards_of in shards:
        steps = jax.random.uniform(jax.random.fold_in(jax.random.fold_in(stream_key, 6), dim), (shards_of,), jnp.float32, smallest / len(shards), top_value / len(shards))
        loudness = loudness * jnp.repeat(jnp.exp(steps), extent[dim] // shards_of).reshape((-1,) + (1,) * (len(extent) - 1 - dim))
    return loudness


def length_profile(count, total, reach, slope):
    loads = [(1 << 20) // math.isqrt(rank ** slope) + 1 for rank in range(2, count + 1)]
    spare, counts = total - reach - (count - 1), [1] * (count - 1)
    while spare > 0:
        candidates = [i for i in range(count - 1) if counts[i] < reach]
        pool, left = sum([loads[i] for i in candidates]), spare
        for i in candidates:
            addition = min(reach - counts[i], max(1, left * loads[i] // pool), spare)
            counts[i] = counts[i] + addition
            spare = spare - addition
    return np.array([reach] + counts)


def ragged_sizes(key, amount, total, bound, slope):
    if amount == 2:
        one = jax.random.randint(key, (), max(1, total - bound), min(bound, total - 1) + 1)
        return jnp.stack([one, total - one])
    lengths = jnp.asarray(length_profile(amount, total, bound, slope), jnp.int32)
    twos = (amount - 1) // 2
    giver, sink = lengths[1:1 + 2 * twos:2], lengths[2:2 + 2 * twos:2]
    slack = jnp.minimum(giver - 1, bound - sink)
    shifted = jax.random.randint(jax.random.fold_in(key, 1), (twos,), 0, 1 << 20) % (slack + 1)
    lengths = lengths.at[1:1 + 2 * twos:2].set(giver - shifted).at[2:2 + 2 * twos:2].set(sink + shifted)
    return lengths[jax.random.permutation(jax.random.fold_in(key, 2), amount)]


def noise(rng, dims, width, reach, cuts=(), held_as=jnp.bfloat16):
    loudness = block_scale(rng, dims, cuts, -0.22, 0.18) if cuts else 1.0
    entries = jax.random.normal(rng, dims, jnp.float32) * width * loudness
    return jnp.minimum(jnp.maximum(entries, -reach), reach).astype(held_as)


def setup_inputs(seed: int = 0) -> dict:
    splits = jax.random.split(jax.random.key(seed), 5)
    amplitudes = noise(splits[0], (OCC_PAIRS, VIRT_PAIRS), 1.0, 6.0, ((0, 512),))
    integrals = noise(splits[1], (VIRT_PAIRS, OUT_PAIRS), (VIRT_PAIRS // IRREPS) ** -0.5, 0.03125, ((0, 64), (1, 8)))
    occ_irreps = touch_ends(jax.random.randint(splits[2], (OCCUPIED,), 0, IRREPS), jax.random.fold_in(splits[2], 1), 0, IRREPS - 1).astype(jnp.int32)
    block_sizes = ragged_sizes(splits[3], IRREPS, VIRTUAL, 2 * VIRTUAL // 5, 1).astype(jnp.int32)
    return {"amplitudes": amplitudes, "integrals": integrals, "occ_irreps": occ_irreps, "block_sizes": block_sizes}


def virtual_labels(block_sizes):
    ends = jnp.cumsum(block_sizes).astype(jnp.int32)
    orbital = jnp.arange(VIRTUAL, dtype=jnp.int32)
    return jnp.sum((orbital[:, None] >= ends[None, :]).astype(jnp.int32), axis=1).astype(jnp.int32)


def reference(amplitudes, integrals, occ_irreps, block_sizes):
    virt_irrep = virtual_labels(block_sizes)
    virt_pair = jnp.bitwise_xor(virt_irrep[:, None], virt_irrep[None, :]).reshape(VIRT_PAIRS)
    pair_ids = jnp.arange(OCC_PAIRS, dtype=jnp.int32)
    occ_pair = jnp.bitwise_xor(occ_irreps[pair_ids // OCCUPIED], occ_irreps[pair_ids % OCCUPIED])
    out_irrep = virt_pair[:OUT_PAIRS]
    amp_three = amplitudes.reshape(OCC_PAIRS, VIRTUAL, VIRTUAL)
    int_three = integrals.reshape(VIRTUAL, VIRTUAL, OUT_PAIRS)

    def advance(running, c_index):
        amp_block = lax.dynamic_index_in_dim(amp_three, c_index, 1, keepdims=False)
        int_block = lax.dynamic_index_in_dim(int_three, c_index, 0, keepdims=False)
        block_irrep = lax.dynamic_slice_in_dim(virt_pair, c_index * VIRTUAL, VIRTUAL)
        kept_amp = jnp.where(occ_pair[:, None] == block_irrep[None, :], amp_block, jnp.zeros_like(amp_block)).astype(jnp.float32)
        kept_int = jnp.where(block_irrep[:, None] == out_irrep[None, :], int_block, jnp.zeros_like(int_block)).astype(jnp.float32)
        return running + jnp.dot(kept_amp, kept_int, precision=lax.Precision.HIGHEST), None

    running, unused = lax.scan(advance, jnp.zeros((OCC_PAIRS, OUT_PAIRS), jnp.float32), jnp.arange(VIRTUAL, dtype=jnp.int32))
    return running.astype(jnp.bfloat16)
```

```python
import jax
import jax.numpy as jnp
from jax import lax
from jax.sharding import PartitionSpec as P

OCCUPIED = 50
VIRTUAL = 400


def virtual_labels(block_sizes):
    ends = jnp.sum(jnp.tril(jnp.ones((4, 4), jnp.int32)) * block_sizes[None, :], axis=1)
    orbital = jnp.arange(VIRTUAL, dtype=jnp.int32)
    return jnp.sum((orbital[:, None] >= ends[None, :]).astype(jnp.int32), axis=1)


def on_device(amplitudes, integrals, occ_irreps, block_sizes):
    row_count = lax.axis_size("row")
    col_count = lax.axis_size("col")
    row_index = lax.axis_index("row")
    col_index = lax.axis_index("col")
    local_pairs = amplitudes.shape[0]
    contracted = integrals.shape[0]
    columns = integrals.shape[1]
    virt_irrep = virtual_labels(block_sizes)
    virt_pair = jnp.bitwise_xor(virt_irrep[:, None], virt_irrep[None, :]).reshape(VIRTUAL * VIRTUAL)
    first_pair = (row_index * col_count + col_index) * local_pairs
    pair_ids = first_pair + jnp.arange(local_pairs, dtype=jnp.int32)
    occ_pair = jnp.bitwise_xor(occ_irreps[pair_ids // OCCUPIED], occ_irreps[pair_ids % OCCUPIED])
    masked = jnp.where(
        occ_pair[:, None] == virt_pair[None, :], amplitudes, jnp.zeros_like(amplitudes)
    )
    regrouped = lax.all_to_all(masked, "row", split_axis=1, concat_axis=0, tiled=True)
    local_irrep = lax.dynamic_slice_in_dim(virt_pair, row_index * contracted, contracted)
    out_irrep = lax.dynamic_slice_in_dim(virt_pair, col_index * columns, columns)
    kept = jnp.where(
        local_irrep[:, None] == out_irrep[None, :], integrals, jnp.zeros_like(integrals)
    )
    partial_value = jnp.dot(
        regrouped,
        lax.all_gather(kept, "col", axis=1, tiled=True),
        preferred_element_type=jnp.float32,
    )
    shaped = partial_value.reshape(row_count, local_pairs * columns * col_count // 128, 128)
    pieces = lax.all_to_all(
        shaped.astype(jnp.bfloat16), "row", split_axis=0, concat_axis=0, tiled=True
    )
    summed = jnp.sum(pieces.astype(jnp.float32), axis=0)
    rounded = summed.reshape(local_pairs, columns * col_count).astype(jnp.bfloat16)
    return lax.all_to_all(rounded, "col", split_axis=1, concat_axis=0, tiled=True)


def solution(mesh):
    in_specs = (P(("row", "col"), None), P("row", "col"), P(), P())
    out_specs = P("row", "col")
    return jax.shard_map(
        on_device, mesh=mesh, in_specs=in_specs, out_specs=out_specs, check_vma=False
    )
```

```python
import jax
import jax.numpy as jnp
from jax import lax
from jax.experimental import pallas as pl
from jax.experimental.pallas import tpu as pltpu
from jax.sharding import Mesh, PartitionSpec as P

OCCUPIED = 50
VIRTUAL = 400
WIDTH = 160
RANGE = 2500
SEGMENTS = 7
WINDOWS = 13
MAIN = 128
REST = WIDTH - MAIN
TILES = 2 * WINDOWS
GROUPS = -(-TILES // 4)
DEPTH = (TILES + GROUPS) * MAIN
PAD = 304
SPAN = 416
BF16 = jnp.bfloat16
F32 = jnp.float32


def block_starts(size_ref):
    starts = [0]
    for k in range(3):
        starts.append(starts[-1] + size_ref[k])
    return starts


def block_of(starts, value):
    label = jnp.where(value >= starts[1], 1, 0)
    label = label + jnp.where(value >= starts[2], 1, 0)
    return label + jnp.where(value >= starts[3], 1, 0)


def column_label(starts, first):
    s = first + lax.broadcasted_iota(jnp.int32, (1, 128), 1)
    a = jnp.where(s >= VIRTUAL, 1, 0) + jnp.where(s >= 2 * VIRTUAL, 1, 0)
    return jnp.bitwise_xor(block_of(starts, a), block_of(starts, s - VIRTUAL * a))


def pack_integrals(place_ref, size_ref, b_ref, out_ref, pad_ref, pick_ref):
    xl, z, co, xh, y = [place_ref[i] for i in range(5)]
    starts = block_starts(size_ref)
    first = RANGE * (xl * 32 + z * 2 + co)
    orbital = first // VIRTUAL
    offset = first - orbital * VIRTUAL
    label = column_label(starts, (xh * 4 + y) * 128)
    whole = RANGE // 16 * 16
    pad_ref[0:PAD] = jnp.zeros((PAD, 128), BF16)
    pad_ref[PAD : PAD + whole] = b_ref[0:whole]
    tail = jnp.concatenate(
        [b_ref[whole:RANGE].astype(F32), jnp.zeros((whole + 16 - RANGE, 128), F32)], axis=0
    )
    pad_ref[PAD + whole : PAD + whole + 16] = tail.astype(BF16)
    rest = pad_ref.shape[0] - (PAD + whole + 16)
    pad_ref[PAD + whole + 16 :] = jnp.zeros((rest, 128), BF16)
    start = (PAD - offset) // 16 * 16
    shift = PAD - offset - start
    t = lax.broadcasted_iota(jnp.int32, (WIDTH, SPAN), 0)
    row = lax.broadcasted_iota(jnp.int32, (WIDTH, SPAN), 1)
    for k in range(4):
        hit = (row == t + (starts[k] + shift)) & (t < size_ref[k])
        pick_ref[k * WIDTH : (k + 1) * WIDTH] = jnp.where(hit, 1.0, 0.0).astype(BF16)
    for j in range(SEGMENTS):
        rows = pad_ref[pl.ds(pl.multiple_of(start + VIRTUAL * j, 16), SPAN), :]
        picked = jnp.dot(pick_ref[...], rows, preferred_element_type=F32)
        want = jnp.bitwise_xor(block_of(starts, orbital + j), label)
        kept = jnp.zeros((WIDTH, 128), F32)
        for k in range(4):
            kept = jnp.where(want == k, picked[k * WIDTH : (k + 1) * WIDTH], kept)
        out_ref[j] = kept.astype(BF16)


def pack_amplitudes(place_ref, size_ref, occ_ref, a_ref, out_ref, pick_ref, main_ref, rest_ref):
    xl, z, co, xh, y = [place_ref[i] for i in range(5)]
    starts = block_starts(size_ref)
    first = (xl * 32 + z * 2 + co) * 16 + (xh * 4 + y) * 2
    d = lax.broadcasted_iota(jnp.int32, (VIRTUAL, 2 * MAIN), 0)
    lane = lax.broadcasted_iota(jnp.int32, (VIRTUAL, 2 * MAIN), 1)
    t = jnp.where(lane < MAIN, lane, MAIN + lane % REST)
    for k in range(4):
        pick_ref[:, 2 * MAIN * k : 2 * MAIN * (k + 1)] = jnp.where(
            d == t + starts[k], 1.0, 0.0
        ).astype(BF16)
    orbital = block_of(starts, lax.broadcasted_iota(jnp.int32, (VIRTUAL, 1), 0))
    group = lax.broadcasted_iota(jnp.int32, (16, MAIN), 1) // REST
    for i in range(2):
        pair = first + i
        label = jnp.bitwise_xor(occ_ref[pair // OCCUPIED], occ_ref[pair % OCCUPIED])
        want = jnp.bitwise_xor(orbital, label)
        picked = jnp.dot(
            a_ref[i * VIRTUAL : (i + 1) * VIRTUAL], pick_ref[...], preferred_element_type=F32
        )
        kept = jnp.zeros((VIRTUAL, 2 * MAIN), F32)
        for k in range(4):
            kept = jnp.where(want == k, picked[:, 2 * MAIN * k : 2 * MAIN * (k + 1)], kept)
        main_ref[...] = kept[:, :MAIN]
        rest_ref[...] = kept[:, MAIN:]
        for v in range(GROUPS):
            packed = jnp.zeros((16, MAIN), F32)
            for m in range(4):
                w = 4 * v + m
                if w >= TILES:
                    continue
                c = w // WINDOWS * 200 + w % WINDOWS
                mains = [main_ref[pl.ds(c + 12 * h, 8, stride=25)] for h in range(2)]
                rests = [rest_ref[pl.ds(c + 12 * h, 8, stride=25)] for h in range(2)]
                out_ref[i, :, MAIN * w : MAIN * (w + 1)] = jnp.concatenate(mains, 0).astype(BF16)
                packed = jnp.where(group == m, jnp.concatenate(rests, 0), packed)
            lo = MAIN * (TILES + v)
            out_ref[i, :, lo : lo + MAIN] = packed.astype(BF16)


def multiply(place_ref, size_ref, label_ref, a_ref, own_ref, other_ref, out_ref, b_ref, sum_ref):
    xl, z, co, xh, y = [place_ref[i] for i in range(5)]
    starts = block_starts(size_ref)
    low = TILES * MAIN
    spare = DEPTH - low - TILES * REST
    b_ref[low + TILES * REST :] = jnp.zeros((spare, 256), BF16)
    for w in (0, 6, 12, 13, 19, 25):
        b_ref[w * MAIN : (w + 1) * MAIN] = jnp.zeros((MAIN, 256), BF16)
        b_ref[low + w * REST : low + (w + 1) * REST] = jnp.zeros((REST, 256), BF16)
    for flip_co, from_ref in ((0, own_ref), (1, other_ref)):
        for flip_xl in range(2):
            base = jnp.bitwise_xor(xl, flip_xl) * WINDOWS + jnp.bitwise_xor(co, flip_co) * 6
            for flip_xh in range(2):
                lanes = slice(flip_xh * 128, (flip_xh + 1) * 128)
                for j in range(SEGMENTS):
                    upper = pl.ds(pl.multiple_of((base + j) * MAIN, MAIN), MAIN)
                    lower = pl.ds(pl.multiple_of(low + (base + j) * REST, REST), REST)
                    head = from_ref[flip_xl, flip_xh, j, 0:MAIN]
                    tail = from_ref[flip_xl, flip_xh, j, MAIN:WIDTH]
                    if j in (0, 6):
                        head = head + b_ref[upper, lanes]
                        tail = tail + b_ref[lower, lanes]
                    b_ref[upper, lanes] = head
                    b_ref[lower, lanes] = tail
    total = jnp.dot(a_ref[...], b_ref[...], preferred_element_type=F32)
    for flip_xh in range(2):
        there = jnp.bitwise_xor(xh, flip_xh)
        label = column_label(starts, (there * 4 + y) * 128)
        part = jnp.where(
            label_ref[...] == label, total[:, flip_xh * 128 : (flip_xh + 1) * 128], 0.0
        )
        sum_ref[...] = part
        for yy in range(4):
            for zz in range(16):
                out_ref[zz, there, 2 * yy : 2 * yy + 2] = sum_ref[
                    32 * yy + 2 * zz : 32 * yy + 2 * zz + 2
                ]


def in_vmem(count):
    return [pl.BlockSpec(memory_space=pltpu.VMEM)] * count


def in_smem(count):
    return [pl.BlockSpec(memory_space=pltpu.SMEM)] * count


def call(kernel, out_shape, out_type, specs, scratch):
    return pl.pallas_call(
        kernel,
        out_shape=jax.ShapeDtypeStruct(out_shape, out_type),
        in_specs=specs,
        out_specs=pl.BlockSpec(memory_space=pltpu.VMEM),
        scratch_shapes=scratch,
        compiler_params=pltpu.CompilerParams(vmem_limit_bytes=40 * 1024 * 1024),
    )


def run_pack_integrals(place, block_sizes, integrals):
    return call(
        pack_integrals,
        (SEGMENTS, WIDTH, 128),
        BF16,
        in_smem(2) + in_vmem(1),
        [pltpu.VMEM((PAD + 6 * VIRTUAL + SPAN, 128), BF16), pltpu.VMEM((4 * WIDTH, SPAN), BF16)],
    )(place, block_sizes, integrals)


def run_pack_amplitudes(place, block_sizes, occ_irreps, amplitudes):
    return call(
        pack_amplitudes,
        (2, 16, DEPTH),
        BF16,
        in_smem(3) + in_vmem(1),
        [
            pltpu.VMEM((VIRTUAL, 8 * MAIN), BF16),
            pltpu.VMEM((VIRTUAL, MAIN), F32),
            pltpu.VMEM((VIRTUAL, MAIN), F32),
        ],
    )(place, block_sizes, occ_irreps, amplitudes.reshape(2 * VIRTUAL, VIRTUAL))


def run_multiply(place, block_sizes, labels, spread, own, other):
    return call(
        multiply,
        (16, 2, 8, 128),
        F32,
        in_smem(2) + in_vmem(4),
        [pltpu.VMEM((DEPTH, 256), BF16), pltpu.VMEM((128, 128), F32)],
    )(place, block_sizes, labels, spread, own, other)


def row_labels(place, occ_irreps):
    row = jnp.arange(128, dtype=jnp.int32)
    xl, z, co, xh, y = [place[i] for i in range(5)]
    pair = xl * 512 + (row // 2 % 16) * 32 + co * 16 + xh * 8 + (row // 32) * 2 + row % 2
    orbitals = jnp.arange(OCCUPIED, dtype=jnp.int32)[None, :]
    irreps = occ_irreps[None, :]
    one = jnp.sum(jnp.where((pair // OCCUPIED)[:, None] == orbitals, irreps, 0), axis=1)
    two = jnp.sum(jnp.where((pair % OCCUPIED)[:, None] == orbitals, irreps, 0), axis=1)
    return jnp.bitwise_xor(one, two)[:, None]


def swap(array, axis):
    return lax.ppermute(array, axis, [(0, 1), (1, 0)])


def on_device(amplitudes, integrals, occ_irreps, block_sizes):
    place = jnp.stack([lax.axis_index(n) for n in ("xl", "z", "co", "xh", "y")]).astype(jnp.int32)
    packed_b = run_pack_integrals(place, block_sizes, integrals)
    pair_b = jnp.stack([packed_b, swap(packed_b, "xh")])
    own_b = jnp.stack([pair_b, swap(pair_b, "xl")])
    other_b = swap(own_b, "co")
    packed_a = run_pack_amplitudes(place, block_sizes, occ_irreps, amplitudes)
    sent = packed_a.reshape(2, 2, 8, DEPTH).transpose(2, 1, 0, 3).reshape(16, 2, DEPTH)
    came = lax.all_to_all(sent, "z", split_axis=0, concat_axis=0, tiled=True)
    copies = jnp.broadcast_to(came.reshape(1, 32, DEPTH), (4, 32, DEPTH))
    spread = lax.all_to_all(copies, "y", split_axis=0, concat_axis=0, tiled=True)
    labels = row_labels(place, occ_irreps)
    parts = run_multiply(place, block_sizes, labels, spread.reshape(128, DEPTH), own_b, other_b)
    pieces = lax.all_to_all(
        parts.reshape(32, 8, 128), ("z", "xh"), split_axis=0, concat_axis=0, tiled=True
    )
    total = jnp.sum(pieces.reshape(16, 2, 8, 128), axis=0)
    return total.reshape(16, 128).astype(BF16)


def solution(mesh):
    split = Mesh(mesh.devices.reshape(2, 16, 2, 2, 4), ("xl", "z", "co", "xh", "y"))
    row, col = ("xl", "z", "co"), ("xh", "y")
    return jax.shard_map(
        on_device,
        mesh=split,
        in_specs=(P(row + col, None), P(row, col), P(), P()),
        out_specs=P(row, col),
        check_vma=False,
    )
```

```python
import jax
import jax.numpy as jnp
from jax import lax
from jax.experimental import pallas as pl
from jax.experimental.pallas import tpu as pltpu
from jax.sharding import Mesh, PartitionSpec as P

OCCUPIED = 50
VIRTUAL = 400
WIDTH = 160
RANGE = 2500
SEGMENTS = 7
WINDOWS = 13
MAIN = 128
REST = WIDTH - MAIN
TILES = 2 * WINDOWS
GROUPS = -(-TILES // 4)
DEPTH = (TILES + GROUPS) * MAIN
PAD = 304
SPAN = 416
BF16 = jnp.bfloat16
F32 = jnp.float32


def block_starts(size_ref):
    starts = [0]
    for k in range(3):
        starts.append(starts[-1] + size_ref[k])
    return starts


def block_of(starts, value):
    label = jnp.where(value >= starts[1], 1, 0)
    label = label + jnp.where(value >= starts[2], 1, 0)
    return label + jnp.where(value >= starts[3], 1, 0)


def column_label(starts, first):
    s = first + lax.broadcasted_iota(jnp.int32, (1, 128), 1)
    a = jnp.where(s >= VIRTUAL, 1, 0) + jnp.where(s >= 2 * VIRTUAL, 1, 0)
    return jnp.bitwise_xor(block_of(starts, a), block_of(starts, s - VIRTUAL * a))


def pack_integrals(place_ref, size_ref, b_ref, out_ref, pad_ref, pick_ref):
    xl, z, co, xh, y = [place_ref[i] for i in range(5)]
    starts = block_starts(size_ref)
    first = RANGE * (xl * 32 + z * 2 + co)
    orbital = first // VIRTUAL
    offset = first - orbital * VIRTUAL
    label = column_label(starts, (xh * 4 + y) * 128)
    whole = RANGE // 16 * 16
    pad_ref[0:PAD] = jnp.zeros((PAD, 128), BF16)
    pad_ref[PAD : PAD + whole] = b_ref[0:whole]
    tail = jnp.concatenate(
        [b_ref[whole:RANGE].astype(F32), jnp.zeros((whole + 16 - RANGE, 128), F32)], axis=0
    )
    pad_ref[PAD + whole : PAD + whole + 16] = tail.astype(BF16)
    rest = pad_ref.shape[0] - (PAD + whole + 16)
    pad_ref[PAD + whole + 16 :] = jnp.zeros((rest, 128), BF16)
    start = (PAD - offset) // 16 * 16
    shift = PAD - offset - start
    t = lax.broadcasted_iota(jnp.int32, (WIDTH, SPAN), 0)
    row = lax.broadcasted_iota(jnp.int32, (WIDTH, SPAN), 1)
    for k in range(4):
        hit = (row == t + (starts[k] + shift)) & (t < size_ref[k])
        pick_ref[k * WIDTH : (k + 1) * WIDTH] = jnp.where(hit, 1.0, 0.0).astype(BF16)
    for j in range(SEGMENTS):
        rows = pad_ref[pl.ds(pl.multiple_of(start + VIRTUAL * j, 16), SPAN), :]
        picked = jnp.dot(pick_ref[...], rows, preferred_element_type=F32)
        want = jnp.bitwise_xor(block_of(starts, orbital + j), label)
        kept = jnp.zeros((WIDTH, 128), F32)
        for k in range(4):
            kept = jnp.where(want == k, picked[k * WIDTH : (k + 1) * WIDTH], kept)
        out_ref[j] = kept.astype(BF16)


def pack_amplitudes(place_ref, size_ref, occ_ref, a_ref, out_ref, pick_ref, main_ref, rest_ref):
    xl, z, co, xh, y = [place_ref[i] for i in range(5)]
    starts = block_starts(size_ref)
    first = (xl * 32 + z * 2 + co) * 16 + (xh * 4 + y) * 2
    d = lax.broadcasted_iota(jnp.int32, (VIRTUAL, 2 * MAIN), 0)
    lane = lax.broadcasted_iota(jnp.int32, (VIRTUAL, 2 * MAIN), 1)
    t = jnp.where(lane < MAIN, lane, MAIN + lane % REST)
    for k in range(4):
        pick_ref[:, 2 * MAIN * k : 2 * MAIN * (k + 1)] = jnp.where(
            d == t + starts[k], 1.0, 0.0
        ).astype(BF16)
    orbital = block_of(starts, lax.broadcasted_iota(jnp.int32, (VIRTUAL, 1), 0))
    group = lax.broadcasted_iota(jnp.int32, (16, MAIN), 1) // REST
    for i in range(2):
        pair = first + i
        label = jnp.bitwise_xor(occ_ref[pair // OCCUPIED], occ_ref[pair % OCCUPIED])
        want = jnp.bitwise_xor(orbital, label)
        picked = jnp.dot(
            a_ref[i * VIRTUAL : (i + 1) * VIRTUAL], pick_ref[...], preferred_element_type=F32
        )
        kept = jnp.zeros((VIRTUAL, 2 * MAIN), F32)
        for k in range(4):
            kept = jnp.where(want == k, picked[:, 2 * MAIN * k : 2 * MAIN * (k + 1)], kept)
        main_ref[...] = kept[:, :MAIN]
        rest_ref[...] = kept[:, MAIN:]
        for v in range(GROUPS):
            packed = jnp.zeros((16, MAIN), F32)
            for m in range(4):
                w = 4 * v + m
                if w >= TILES:
                    continue
                c = w // WINDOWS * 200 + w % WINDOWS
                mains = [main_ref[pl.ds(c + 12 * h, 8, stride=25)] for h in range(2)]
                rests = [rest_ref[pl.ds(c + 12 * h, 8, stride=25)] for h in range(2)]
                out_ref[i, :, MAIN * w : MAIN * (w + 1)] = jnp.concatenate(mains, 0).astype(BF16)
                packed = jnp.where(group == m, jnp.concatenate(rests, 0), packed)
            lo = MAIN * (TILES + v)
            out_ref[i, :, lo : lo + MAIN] = packed.astype(BF16)


def multiply(place_ref, size_ref, label_ref, a_ref, own_ref, other_ref, out_ref, b_ref, sum_ref):
    xl, z, co, xh, y = [place_ref[i] for i in range(5)]
    starts = block_starts(size_ref)
    low = TILES * MAIN
    spare = DEPTH - low - TILES * REST
    b_ref[low + TILES * REST :] = jnp.zeros((spare, 256), BF16)
    for w in (0, 6, 12, 13, 19, 25):
        b_ref[w * MAIN : (w + 1) * MAIN] = jnp.zeros((MAIN, 256), BF16)
        b_ref[low + w * REST : low + (w + 1) * REST] = jnp.zeros((REST, 256), BF16)
    for flip_co, from_ref in ((0, own_ref), (1, other_ref)):
        for flip_xl in range(2):
            base = jnp.bitwise_xor(xl, flip_xl) * WINDOWS + jnp.bitwise_xor(co, flip_co) * 6
            for flip_xh in range(2):
                lanes = slice(flip_xh * 128, (flip_xh + 1) * 128)
                for j in range(SEGMENTS):
                    upper = pl.ds(pl.multiple_of((base + j) * MAIN, MAIN), MAIN)
                    lower = pl.ds(pl.multiple_of(low + (base + j) * REST, REST), REST)
                    head = from_ref[flip_xl, flip_xh, j, 0:MAIN]
                    tail = from_ref[flip_xl, flip_xh, j, MAIN:WIDTH]
                    if j in (0, 6):
                        head = head + b_ref[upper, lanes]
                        tail = tail + b_ref[lower, lanes]
                    b_ref[upper, lanes] = head
                    b_ref[lower, lanes] = tail
    total = jnp.dot(a_ref[...], b_ref[...], preferred_element_type=F32)
    for flip_xh in range(2):
        there = jnp.bitwise_xor(xh, flip_xh)
        label = column_label(starts, (there * 4 + y) * 128)
        part = jnp.where(
            label_ref[...] == label, total[:, flip_xh * 128 : (flip_xh + 1) * 128], 0.0
        )
        sum_ref[...] = part
        for yy in range(4):
            for zz in range(16):
                out_ref[zz, there, 2 * yy : 2 * yy + 2] = sum_ref[
                    32 * yy + 2 * zz : 32 * yy + 2 * zz + 2
                ]


def in_vmem(count):
    return [pl.BlockSpec(memory_space=pltpu.VMEM)] * count


def in_smem(count):
    return [pl.BlockSpec(memory_space=pltpu.SMEM)] * count


def call(kernel, out_shape, out_type, specs, scratch):
    return pl.pallas_call(
        kernel,
        out_shape=jax.ShapeDtypeStruct(out_shape, out_type),
        in_specs=specs,
        out_specs=pl.BlockSpec(memory_space=pltpu.VMEM),
        scratch_shapes=scratch,
        compiler_params=pltpu.CompilerParams(vmem_limit_bytes=40 * 1024 * 1024),
    )


def run_pack_integrals(place, block_sizes, integrals):
    return call(
        pack_integrals,
        (SEGMENTS, WIDTH, 128),
        BF16,
        in_smem(2) + in_vmem(1),
        [pltpu.VMEM((PAD + 6 * VIRTUAL + SPAN, 128), BF16), pltpu.VMEM((4 * WIDTH, SPAN), BF16)],
    )(place, block_sizes, integrals)


def run_pack_amplitudes(place, block_sizes, occ_irreps, amplitudes):
    return call(
        pack_amplitudes,
        (2, 16, DEPTH),
        BF16,
        in_smem(3) + in_vmem(1),
        [
            pltpu.VMEM((VIRTUAL, 8 * MAIN), BF16),
            pltpu.VMEM((VIRTUAL, MAIN), F32),
            pltpu.VMEM((VIRTUAL, MAIN), F32),
        ],
    )(place, block_sizes, occ_irreps, amplitudes.reshape(2 * VIRTUAL, VIRTUAL))


def run_multiply(place, block_sizes, labels, spread, own, other):
    return call(
        multiply,
        (16, 2, 8, 128),
        F32,
        in_smem(2) + in_vmem(4),
        [pltpu.VMEM((DEPTH, 256), BF16), pltpu.VMEM((128, 128), F32)],
    )(place, block_sizes, labels, spread, own, other)


def row_labels(place, occ_irreps):
    row = jnp.arange(128, dtype=jnp.int32)
    xl, z, co, xh, y = [place[i] for i in range(5)]
    pair = xl * 512 + (row // 2 % 16) * 32 + co * 16 + xh * 8 + (row // 32) * 2 + row % 2
    orbitals = jnp.arange(OCCUPIED, dtype=jnp.int32)[None, :]
    irreps = occ_irreps[None, :]
    one = jnp.sum(jnp.where((pair // OCCUPIED)[:, None] == orbitals, irreps, 0), axis=1)
    two = jnp.sum(jnp.where((pair % OCCUPIED)[:, None] == orbitals, irreps, 0), axis=1)
    return jnp.bitwise_xor(one, two)[:, None]


def swap(array, axis):
    return lax.ppermute(array, axis, [(0, 1), (1, 0)])


def on_device(amplitudes, integrals, occ_irreps, block_sizes):
    place = jnp.stack([lax.axis_index(n) for n in ("xl", "z", "co", "xh", "y")]).astype(jnp.int32)
    packed_b = run_pack_integrals(place, block_sizes, integrals)
    swapped_b = swap(packed_b, "xh")
    amplitudes, packed_b = lax.optimization_barrier((amplitudes, packed_b))
    packed_a = run_pack_amplitudes(place, block_sizes, occ_irreps, amplitudes)
    sent = packed_a.reshape(2, 2, 8, DEPTH).transpose(2, 1, 0, 3).reshape(16, 2, DEPTH)
    sent, packed_b = lax.optimization_barrier((sent, packed_b))
    pair_b = jnp.stack([packed_b, swapped_b])
    sent, pair_b = lax.optimization_barrier((sent, pair_b))
    came = lax.all_to_all(sent, "z", split_axis=0, concat_axis=0, tiled=True)
    swapped_b = swap(pair_b, "xl")
    own_b = jnp.stack([pair_b, swapped_b])
    other_b = swap(own_b, "co")
    copies = jnp.broadcast_to(came.reshape(1, 32, DEPTH), (4, 32, DEPTH))
    spread = lax.all_to_all(copies, "y", split_axis=0, concat_axis=0, tiled=True)
    labels = row_labels(place, occ_irreps)
    parts = run_multiply(place, block_sizes, labels, spread.reshape(128, DEPTH), own_b, other_b)
    pieces = lax.all_to_all(
        parts.reshape(32, 8, 128), ("z", "xh"), split_axis=0, concat_axis=0, tiled=True
    )
    total = jnp.sum(pieces.reshape(16, 2, 8, 128), axis=0)
    return total.reshape(16, 128).astype(BF16)


def solution(mesh):
    split = Mesh(mesh.devices.reshape(2, 16, 2, 2, 4), ("xl", "z", "co", "xh", "y"))
    row, col = ("xl", "z", "co"), ("xh", "y")
    return jax.shard_map(
        on_device,
        mesh=split,
        in_specs=(P(row + col, None), P(row, col), P(), P()),
        out_specs=P(row, col),
        check_vma=False,
    )
```

```python
import jax
import jax.numpy as jnp
from jax import lax
from jax.experimental import pallas as pl
from jax.experimental.pallas import tpu as pltpu
from jax.sharding import Mesh, PartitionSpec as P

OCCUPIED = 50
VIRTUAL = 400
WIDTH = 160
RANGE = 2500
SEGMENTS = 7
WINDOWS = 13
MAIN = 128
REST = WIDTH - MAIN
TILES = 2 * WINDOWS
GROUPS = -(-TILES // 4)
DEPTH = (TILES + GROUPS) * MAIN
PAD = 304
SPAN = 416
BF16 = jnp.bfloat16
F32 = jnp.float32


def block_starts(size_ref):
    starts = [0]
    for k in range(3):
        starts.append(starts[-1] + size_ref[k])
    return starts


def block_of(starts, value):
    label = jnp.where(value >= starts[1], 1, 0)
    label = label + jnp.where(value >= starts[2], 1, 0)
    return label + jnp.where(value >= starts[3], 1, 0)


def column_label(starts, first):
    s = first + lax.broadcasted_iota(jnp.int32, (1, 128), 1)
    a = jnp.where(s >= VIRTUAL, 1, 0) + jnp.where(s >= 2 * VIRTUAL, 1, 0)
    return jnp.bitwise_xor(block_of(starts, a), block_of(starts, s - VIRTUAL * a))


def pack_integrals(place_ref, size_ref, b_ref, out_ref, pad_ref, pick_ref):
    xl, z, co, xh, y = [place_ref[i] for i in range(5)]
    starts = block_starts(size_ref)
    first = RANGE * (xl * 32 + z * 2 + co)
    orbital = first // VIRTUAL
    offset = first - orbital * VIRTUAL
    label = column_label(starts, (xh * 4 + y) * 128)
    whole = RANGE // 16 * 16
    pad_ref[0:PAD] = jnp.zeros((PAD, 128), BF16)
    pad_ref[PAD : PAD + whole] = b_ref[0:whole]
    tail = jnp.concatenate(
        [b_ref[whole:RANGE].astype(F32), jnp.zeros((whole + 16 - RANGE, 128), F32)], axis=0
    )
    pad_ref[PAD + whole : PAD + whole + 16] = tail.astype(BF16)
    rest = pad_ref.shape[0] - (PAD + whole + 16)
    pad_ref[PAD + whole + 16 :] = jnp.zeros((rest, 128), BF16)
    start = (PAD - offset) // 16 * 16
    shift = PAD - offset - start
    t = lax.broadcasted_iota(jnp.int32, (WIDTH, SPAN), 0)
    row = lax.broadcasted_iota(jnp.int32, (WIDTH, SPAN), 1)
    for k in range(4):
        hit = (row == t + (starts[k] + shift)) & (t < size_ref[k])
        pick_ref[k * WIDTH : (k + 1) * WIDTH] = jnp.where(hit, 1.0, 0.0).astype(BF16)
    for j in range(SEGMENTS):
        rows = pad_ref[pl.ds(pl.multiple_of(start + VIRTUAL * j, 16), SPAN), :]
        picked = jnp.dot(pick_ref[...], rows, preferred_element_type=F32)
        want = jnp.bitwise_xor(block_of(starts, orbital + j), label)
        kept = jnp.zeros((WIDTH, 128), F32)
        for k in range(4):
            kept = jnp.where(want == k, picked[k * WIDTH : (k + 1) * WIDTH], kept)
        out_ref[j] = kept.astype(BF16)


def pack_amplitudes(place_ref, size_ref, occ_ref, a_ref, out_ref, pick_ref, main_ref, rest_ref):
    xl, z, co, xh, y = [place_ref[i] for i in range(5)]
    starts = block_starts(size_ref)
    first = (xl * 32 + z * 2 + co) * 16 + (xh * 4 + y) * 2
    d = lax.broadcasted_iota(jnp.int32, (VIRTUAL, 2 * MAIN), 0)
    lane = lax.broadcasted_iota(jnp.int32, (VIRTUAL, 2 * MAIN), 1)
    t = jnp.where(lane < MAIN, lane, MAIN + lane % REST)
    for k in range(4):
        pick_ref[:, 2 * MAIN * k : 2 * MAIN * (k + 1)] = jnp.where(
            d == t + starts[k], 1.0, 0.0
        ).astype(BF16)
    orbital = block_of(starts, lax.broadcasted_iota(jnp.int32, (VIRTUAL, 1), 0))
    group = lax.broadcasted_iota(jnp.int32, (16, MAIN), 1) // REST
    for i in range(2):
        pair = first + i
        label = jnp.bitwise_xor(occ_ref[pair // OCCUPIED], occ_ref[pair % OCCUPIED])
        want = jnp.bitwise_xor(orbital, label)
        picked = jnp.dot(
            a_ref[i * VIRTUAL : (i + 1) * VIRTUAL], pick_ref[...], preferred_element_type=F32
        )
        kept = jnp.zeros((VIRTUAL, 2 * MAIN), F32)
        for k in range(4):
            kept = jnp.where(want == k, picked[:, 2 * MAIN * k : 2 * MAIN * (k + 1)], kept)
        main_ref[...] = kept[:, :MAIN]
        rest_ref[...] = kept[:, MAIN:]
        for v in range(GROUPS):
            packed = jnp.zeros((16, MAIN), F32)
            for m in range(4):
                w = 4 * v + m
                if w >= TILES:
                    continue
                c = w // WINDOWS * 200 + w % WINDOWS
                mains = [main_ref[pl.ds(c + 12 * h, 8, stride=25)] for h in range(2)]
                rests = [rest_ref[pl.ds(c + 12 * h, 8, stride=25)] for h in range(2)]
                out_ref[i, :, MAIN * w : MAIN * (w + 1)] = jnp.concatenate(mains, 0).astype(BF16)
                packed = jnp.where(group == m, jnp.concatenate(rests, 0), packed)
            lo = MAIN * (TILES + v)
            out_ref[i, :, lo : lo + MAIN] = packed.astype(BF16)


def multiply(place_ref, size_ref, label_ref, a_ref, b00_ref, b01_ref, b10_ref, b11_ref, out_ref, b_ref, sum_ref):
    xl, z, co, xh, y = [place_ref[i] for i in range(5)]
    starts = block_starts(size_ref)
    low = TILES * MAIN
    spare = DEPTH - low - TILES * REST
    b_ref[low + TILES * REST :] = jnp.zeros((spare, 256), BF16)
    for w in (0, 6, 12, 13, 19, 25):
        b_ref[w * MAIN : (w + 1) * MAIN] = jnp.zeros((MAIN, 256), BF16)
        b_ref[low + w * REST : low + (w + 1) * REST] = jnp.zeros((REST, 256), BF16)
    for flip_co, refs in ((0, (b00_ref, b10_ref)), (1, (b01_ref, b11_ref))):
        for flip_xl, from_ref in enumerate(refs):
            base = jnp.bitwise_xor(xl, flip_xl) * WINDOWS + jnp.bitwise_xor(co, flip_co) * 6
            for flip_xh in range(2):
                lanes = slice(flip_xh * 128, (flip_xh + 1) * 128)
                for j in range(SEGMENTS):
                    upper = pl.ds(pl.multiple_of((base + j) * MAIN, MAIN), MAIN)
                    lower = pl.ds(pl.multiple_of(low + (base + j) * REST, REST), REST)
                    head = from_ref[flip_xh, j, 0:MAIN]
                    tail = from_ref[flip_xh, j, MAIN:WIDTH]
                    if j in (0, 6):
                        head = head + b_ref[upper, lanes]
                        tail = tail + b_ref[lower, lanes]
                    b_ref[upper, lanes] = head
                    b_ref[lower, lanes] = tail
    total = jnp.dot(a_ref[...], b_ref[...], preferred_element_type=F32)
    for flip_xh in range(2):
        there = jnp.bitwise_xor(xh, flip_xh)
        label = column_label(starts, (there * 4 + y) * 128)
        part = jnp.where(
            label_ref[...] == label, total[:, flip_xh * 128 : (flip_xh + 1) * 128], 0.0
        )
        sum_ref[...] = part
        for yy in range(4):
            for zz in range(16):
                out_ref[zz, there, 2 * yy : 2 * yy + 2] = sum_ref[
                    32 * yy + 2 * zz : 32 * yy + 2 * zz + 2
                ]


def in_vmem(count):
    return [pl.BlockSpec(memory_space=pltpu.VMEM)] * count


def in_smem(count):
    return [pl.BlockSpec(memory_space=pltpu.SMEM)] * count


def call(kernel, out_shape, out_type, specs, scratch):
    return pl.pallas_call(
        kernel,
        out_shape=jax.ShapeDtypeStruct(out_shape, out_type),
        in_specs=specs,
        out_specs=pl.BlockSpec(memory_space=pltpu.VMEM),
        scratch_shapes=scratch,
        compiler_params=pltpu.CompilerParams(vmem_limit_bytes=40 * 1024 * 1024),
    )


def run_pack_integrals(place, block_sizes, integrals):
    return call(
        pack_integrals,
        (SEGMENTS, WIDTH, 128),
        BF16,
        in_smem(2) + in_vmem(1),
        [pltpu.VMEM((PAD + 6 * VIRTUAL + SPAN, 128), BF16), pltpu.VMEM((4 * WIDTH, SPAN), BF16)],
    )(place, block_sizes, integrals)


def run_pack_amplitudes(place, block_sizes, occ_irreps, amplitudes):
    return call(
        pack_amplitudes,
        (2, 16, DEPTH),
        BF16,
        in_smem(3) + in_vmem(1),
        [
            pltpu.VMEM((VIRTUAL, 8 * MAIN), BF16),
            pltpu.VMEM((VIRTUAL, MAIN), F32),
            pltpu.VMEM((VIRTUAL, MAIN), F32),
        ],
    )(place, block_sizes, occ_irreps, amplitudes.reshape(2 * VIRTUAL, VIRTUAL))


def run_multiply(place, block_sizes, labels, spread, blocks):
    return call(
        multiply,
        (16, 2, 8, 128),
        F32,
        in_smem(2) + in_vmem(6),
        [pltpu.VMEM((DEPTH, 256), BF16), pltpu.VMEM((128, 128), F32)],
    )(place, block_sizes, labels, spread, *blocks)


def row_labels(place, occ_irreps):
    row = jnp.arange(128, dtype=jnp.int32)
    xl, z, co, xh, y = [place[i] for i in range(5)]
    pair = xl * 512 + (row // 2 % 16) * 32 + co * 16 + xh * 8 + (row // 32) * 2 + row % 2
    orbitals = jnp.arange(OCCUPIED, dtype=jnp.int32)[None, :]
    irreps = occ_irreps[None, :]
    one = jnp.sum(jnp.where((pair // OCCUPIED)[:, None] == orbitals, irreps, 0), axis=1)
    two = jnp.sum(jnp.where((pair % OCCUPIED)[:, None] == orbitals, irreps, 0), axis=1)
    return jnp.bitwise_xor(one, two)[:, None]


def swap(array, axis):
    return lax.ppermute(array, axis, [(0, 1), (1, 0)])


def on_device(amplitudes, integrals, occ_irreps, block_sizes):
    place = jnp.stack([lax.axis_index(n) for n in ("xl", "z", "co", "xh", "y")]).astype(jnp.int32)
    packed_a = run_pack_amplitudes(place, block_sizes, occ_irreps, amplitudes)
    sent = packed_a.reshape(2, 2, 8, DEPTH).transpose(2, 1, 0, 3).reshape(16, 2, DEPTH)
    sent, integrals = lax.optimization_barrier((sent, integrals))
    came = lax.all_to_all(sent, "z", split_axis=0, concat_axis=0, tiled=True)
    packed_b = run_pack_integrals(place, block_sizes, integrals)
    pair_b = jnp.stack([packed_b, swap(packed_b, "xh")])
    far_b = swap(pair_b, "xl")
    copies = jnp.broadcast_to(came.reshape(1, 32, DEPTH), (4, 32, DEPTH))
    spread = lax.all_to_all(copies, "y", split_axis=0, concat_axis=0, tiled=True)
    blocks_b = [pair_b, swap(pair_b, "co"), far_b, swap(far_b, "co")]
    labels = row_labels(place, occ_irreps)
    parts = run_multiply(place, block_sizes, labels, spread.reshape(128, DEPTH), blocks_b)
    pieces = lax.all_to_all(
        parts.reshape(32, 8, 128), ("z", "xh"), split_axis=0, concat_axis=0, tiled=True
    )
    total = jnp.sum(pieces.reshape(16, 2, 8, 128), axis=0)
    return total.reshape(16, 128).astype(BF16)


def solution(mesh):
    split = Mesh(mesh.devices.reshape(2, 16, 2, 2, 4), ("xl", "z", "co", "xh", "y"))
    row, col = ("xl", "z", "co"), ("xh", "y")
    return jax.shard_map(
        on_device,
        mesh=split,
        in_specs=(P(row + col, None), P(row, col), P(), P()),
        out_specs=P(row, col),
        check_vma=False,
    )
```

```python
import jax
import jax.numpy as jnp
from jax import lax
from jax.experimental import pallas as pl
from jax.experimental.pallas import tpu as pltpu
from jax.sharding import Mesh, PartitionSpec as P

OCCUPIED = 50
VIRTUAL = 400
WIDTH = 160
RANGE = 2500
SEGMENTS = 7
WINDOWS = 13
MAIN = 128
REST = WIDTH - MAIN
TILES = 2 * WINDOWS
GROUPS = -(-TILES // 4)
DEPTH = (TILES + GROUPS) * MAIN
PAD = 304
BF16 = jnp.bfloat16
F32 = jnp.float32


def block_starts(size_ref):
    starts = [0]
    for k in range(3):
        starts.append(starts[-1] + size_ref[k])
    return starts


def block_of(starts, value):
    label = jnp.where(value >= starts[1], 1, 0)
    label = label + jnp.where(value >= starts[2], 1, 0)
    return label + jnp.where(value >= starts[3], 1, 0)


def column_label(starts, first):
    s = first + lax.broadcasted_iota(jnp.int32, (1, 128), 1)
    a = jnp.where(s >= VIRTUAL, 1, 0) + jnp.where(s >= 2 * VIRTUAL, 1, 0)
    return jnp.bitwise_xor(block_of(starts, a), block_of(starts, s - VIRTUAL * a))


def pack_integrals(place_ref, size_ref, b_ref, out_ref, pad_ref):
    xl, z, co, xh, y = [place_ref[i] for i in range(5)]
    starts = block_starts(size_ref)
    first = RANGE * (xl * 32 + z * 2 + co)
    orbital = first // VIRTUAL
    offset = first - orbital * VIRTUAL
    label = column_label(starts, (xh * 4 + y) * 128)
    after = pad_ref.shape[0] - PAD - RANGE
    pad_ref[0:PAD] = jnp.zeros((PAD, 128), F32)
    pad_ref[PAD + RANGE :] = jnp.zeros((after, 128), F32)
    pad_ref[PAD : PAD + RANGE] = b_ref[...].astype(F32)
    t = lax.broadcasted_iota(jnp.int32, (WIDTH, 128), 0)
    for j in range(SEGMENTS):
        want = jnp.bitwise_xor(block_of(starts, orbital + j), label)
        kept = jnp.zeros((WIDTH, 128), F32)
        length = jnp.zeros((1, 128), jnp.int32)
        for k in range(4):
            rows = pad_ref[pl.ds(PAD - offset + VIRTUAL * j + starts[k], WIDTH), :]
            kept = jnp.where(want == k, rows, kept)
            length = jnp.where(want == k, size_ref[k], length)
        out_ref[j] = jnp.where(t < length, kept, 0.0).astype(BF16)


def pack_amplitudes(place_ref, size_ref, occ_ref, a_ref, out_ref, pick_ref, main_ref, rest_ref):
    xl, z, co, xh, y = [place_ref[i] for i in range(5)]
    starts = block_starts(size_ref)
    first = (xl * 32 + z * 2 + co) * 16 + (xh * 4 + y) * 2
    d = lax.broadcasted_iota(jnp.int32, (VIRTUAL, 2 * MAIN), 0)
    lane = lax.broadcasted_iota(jnp.int32, (VIRTUAL, 2 * MAIN), 1)
    t = jnp.where(lane < MAIN, lane, MAIN + lane % REST)
    for k in range(4):
        pick_ref[:, 2 * MAIN * k : 2 * MAIN * (k + 1)] = jnp.where(
            d == t + starts[k], 1.0, 0.0
        ).astype(BF16)
    orbital = block_of(starts, lax.broadcasted_iota(jnp.int32, (VIRTUAL, 1), 0))
    group = lax.broadcasted_iota(jnp.int32, (16, MAIN), 1) // REST
    for i in range(2):
        pair = first + i
        label = jnp.bitwise_xor(occ_ref[pair // OCCUPIED], occ_ref[pair % OCCUPIED])
        want = jnp.bitwise_xor(orbital, label)
        picked = jnp.dot(
            a_ref[i * VIRTUAL : (i + 1) * VIRTUAL], pick_ref[...], preferred_element_type=F32
        )
        kept = jnp.zeros((VIRTUAL, 2 * MAIN), F32)
        for k in range(4):
            kept = jnp.where(want == k, picked[:, 2 * MAIN * k : 2 * MAIN * (k + 1)], kept)
        main_ref[...] = kept[:, :MAIN]
        rest_ref[...] = kept[:, MAIN:]
        for v in range(GROUPS):
            packed = jnp.zeros((16, MAIN), F32)
            for m in range(4):
                w = 4 * v + m
                if w >= TILES:
                    continue
                c = w // WINDOWS * 200 + w % WINDOWS
                places = [pl.ds(c + 12 * h + 25 * u, 4, stride=25) for h in range(2) for u in (4, 0)]
                mains = [main_ref[rows] for rows in places]
                rests = [rest_ref[rows] for rows in places]
                out_ref[i, :, MAIN * w : MAIN * (w + 1)] = jnp.concatenate(mains, 0).astype(BF16)
                packed = jnp.where(group == m, jnp.concatenate(rests, 0), packed)
            lo = MAIN * (TILES + v)
            out_ref[i, :, lo : lo + MAIN] = packed.astype(BF16)


def multiply(place_ref, size_ref, label_ref, a_ref, b00_ref, b01_ref, b10_ref, b11_ref, out_ref, b_ref, sum_ref):
    xl, z, co, xh, y = [place_ref[i] for i in range(5)]
    starts = block_starts(size_ref)
    low = TILES * MAIN
    spare = DEPTH - low - TILES * REST
    b_ref[low + TILES * REST :] = jnp.zeros((spare, 256), BF16)
    for w in (0, 6, 12, 13, 19, 25):
        b_ref[w * MAIN : (w + 1) * MAIN] = jnp.zeros((MAIN, 256), BF16)
        b_ref[low + w * REST : low + (w + 1) * REST] = jnp.zeros((REST, 256), BF16)
    for flip_co, refs in ((0, (b00_ref, b10_ref)), (1, (b01_ref, b11_ref))):
        for flip_xl, from_ref in enumerate(refs):
            base = jnp.bitwise_xor(xl, flip_xl) * WINDOWS + jnp.bitwise_xor(co, flip_co) * 6
            for flip_xh in range(2):
                lanes = slice(flip_xh * 128, (flip_xh + 1) * 128)
                for j in range(SEGMENTS):
                    upper = pl.ds(pl.multiple_of((base + j) * MAIN, MAIN), MAIN)
                    lower = pl.ds(pl.multiple_of(low + (base + j) * REST, REST), REST)
                    head = from_ref[flip_xh, j, 0:MAIN]
                    tail = from_ref[flip_xh, j, MAIN:WIDTH]
                    if j in (0, 6):
                        head = head + b_ref[upper, lanes]
                        tail = tail + b_ref[lower, lanes]
                    b_ref[upper, lanes] = head
                    b_ref[lower, lanes] = tail
    total = jnp.dot(a_ref[...], b_ref[...], preferred_element_type=F32)
    for flip_xh in range(2):
        there = jnp.bitwise_xor(xh, flip_xh)
        label = column_label(starts, (there * 4 + y) * 128)
        part = jnp.where(
            label_ref[...] == label, total[:, flip_xh * 128 : (flip_xh + 1) * 128], 0.0
        )
        sum_ref[...] = part
        for yy in range(4):
            for zz in range(16):
                out_ref[(zz + 8) % 16, there, 2 * yy : 2 * yy + 2] = sum_ref[
                    32 * yy + 2 * zz : 32 * yy + 2 * zz + 2
                ]


def in_vmem(count):
    return [pl.BlockSpec(memory_space=pltpu.VMEM)] * count


def in_smem(count):
    return [pl.BlockSpec(memory_space=pltpu.SMEM)] * count


def call(kernel, out_shape, out_type, specs, scratch):
    return pl.pallas_call(
        kernel,
        out_shape=jax.ShapeDtypeStruct(out_shape, out_type),
        in_specs=specs,
        out_specs=pl.BlockSpec(memory_space=pltpu.VMEM),
        scratch_shapes=scratch,
        compiler_params=pltpu.CompilerParams(vmem_limit_bytes=40 * 1024 * 1024),
    )


def run_pack_integrals(place, block_sizes, integrals):
    return call(
        pack_integrals,
        (SEGMENTS, WIDTH, 128),
        BF16,
        in_smem(2) + in_vmem(1),
        [pltpu.VMEM((PAD + SEGMENTS * VIRTUAL + WIDTH, 128), F32)],
    )(place, block_sizes, integrals)


def run_pack_amplitudes(place, block_sizes, occ_irreps, amplitudes):
    return call(
        pack_amplitudes,
        (2, 16, DEPTH),
        BF16,
        in_smem(3) + in_vmem(1),
        [
            pltpu.VMEM((VIRTUAL, 8 * MAIN), BF16),
            pltpu.VMEM((VIRTUAL, MAIN), F32),
            pltpu.VMEM((VIRTUAL, MAIN), F32),
        ],
    )(place, block_sizes, occ_irreps, amplitudes.reshape(2 * VIRTUAL, VIRTUAL))


def run_multiply(place, block_sizes, labels, spread, blocks):
    return call(
        multiply,
        (16, 2, 8, 128),
        F32,
        in_smem(2) + in_vmem(6),
        [pltpu.VMEM((DEPTH, 256), BF16), pltpu.VMEM((128, 128), F32)],
    )(place, block_sizes, labels, spread, *blocks)


def row_labels(place, occ_irreps):
    row = jnp.arange(128, dtype=jnp.int32)
    xl, z, co, xh, y = [place[i] for i in range(5)]
    pair = xl * 512 + ((row // 2 + 8) % 16) * 32 + co * 16 + xh * 8 + (row // 32) * 2 + row % 2
    orbitals = jnp.arange(OCCUPIED, dtype=jnp.int32)[None, :]
    irreps = occ_irreps[None, :]
    one = jnp.sum(jnp.where((pair // OCCUPIED)[:, None] == orbitals, irreps, 0), axis=1)
    two = jnp.sum(jnp.where((pair % OCCUPIED)[:, None] == orbitals, irreps, 0), axis=1)
    return jnp.bitwise_xor(one, two)[:, None]


def swap(array, axis):
    return lax.ppermute(array, axis, [(0, 1), (1, 0)])


def on_device(amplitudes, integrals, occ_irreps, block_sizes):
    place = jnp.stack([lax.axis_index(n) for n in ("xl", "z", "co", "xh", "y")]).astype(jnp.int32)
    packed_a = run_pack_amplitudes(place, block_sizes, occ_irreps, amplitudes)
    sent = packed_a.reshape(2, 2, 8, DEPTH).transpose(2, 1, 0, 3).reshape(16, 2, DEPTH)
    sent, integrals = lax.optimization_barrier((sent, integrals))
    came = lax.all_to_all(
        sent, "z", split_axis=0, concat_axis=0, tiled=True, axis_index_groups=[[(i + 8) % 16 for i in range(16)]]
    )
    packed_b = run_pack_integrals(place, block_sizes, integrals)
    pair_b = jnp.stack([packed_b, swap(packed_b, "xh")])
    far_b = swap(pair_b, "xl")
    copies = jnp.broadcast_to(came.reshape(1, 32, DEPTH), (4, 32, DEPTH))
    spread = lax.all_to_all(copies, "y", split_axis=0, concat_axis=0, tiled=True)
    blocks_b = [pair_b, swap(pair_b, "co"), far_b, swap(far_b, "co")]
    labels = row_labels(place, occ_irreps)
    parts = run_multiply(place, block_sizes, labels, spread.reshape(128, DEPTH), blocks_b)
    pieces = lax.all_to_all(
        parts.reshape(32, 8, 128), ("z", "xh"), split_axis=0, concat_axis=0, tiled=True
    )
    total = jnp.sum(pieces.reshape(16, 2, 8, 128), axis=0)
    return total.reshape(16, 128).astype(BF16)


def solution(mesh):
    split = Mesh(mesh.devices.reshape(2, 16, 2, 2, 4), ("xl", "z", "co", "xh", "y"))
    row, col = ("xl", "z", "co"), ("xh", "y")
    return jax.shard_map(
        on_device,
        mesh=split,
        in_specs=(P(row + col, None), P(row, col), P(), P()),
        out_specs=P(row, col),
        check_vma=False,
    )
```

```python
import jax
import jax.numpy as jnp
from jax import lax
from jax.experimental import pallas as pl
from jax.experimental.pallas import tpu as pltpu
from jax.sharding import Mesh, PartitionSpec as P

OCCUPIED = 50
VIRTUAL = 400
WIDTH = 160
RANGE = 2500
SEGMENTS = 7
WINDOWS = 13
MAIN = 128
REST = WIDTH - MAIN
TILES = 2 * WINDOWS
GROUPS = -(-TILES // 4)
DEPTH = (TILES + GROUPS) * MAIN
PAD = 304
PITCH = 64
BF16 = jnp.bfloat16
F32 = jnp.float32


def block_starts(size_ref):
    starts = [0]
    for k in range(3):
        starts.append(starts[-1] + size_ref[k])
    return starts


def block_of(starts, value):
    label = jnp.where(value >= starts[1], 1, 0)
    label = label + jnp.where(value >= starts[2], 1, 0)
    return label + jnp.where(value >= starts[3], 1, 0)


def column_label(starts, first):
    s = first + lax.broadcasted_iota(jnp.int32, (1, 128), 1)
    a = jnp.where(s >= VIRTUAL, 1, 0) + jnp.where(s >= 2 * VIRTUAL, 1, 0)
    return jnp.bitwise_xor(block_of(starts, a), block_of(starts, s - VIRTUAL * a))


def pack_integrals(place_ref, size_ref, b_ref, out_ref, pad_ref):
    xl, z, co, xh, y = [place_ref[i] for i in range(5)]
    starts = block_starts(size_ref)
    first = RANGE * (xl * 32 + z * 2 + co)
    orbital = first // VIRTUAL
    offset = first - orbital * VIRTUAL
    label = column_label(starts, (xh * 4 + y) * 128)
    after = pad_ref.shape[0] - PAD - RANGE
    pad_ref[0:PAD] = jnp.zeros((PAD, 128), F32)
    pad_ref[PAD + RANGE :] = jnp.zeros((after, 128), F32)
    pad_ref[PAD : PAD + RANGE] = b_ref[...].astype(F32)
    t = lax.broadcasted_iota(jnp.int32, (WIDTH, 128), 0)
    for j in range(SEGMENTS):
        want = jnp.bitwise_xor(block_of(starts, orbital + j), label)
        kept = jnp.zeros((WIDTH, 128), F32)
        length = jnp.zeros((1, 128), jnp.int32)
        for k in range(4):
            rows = pad_ref[pl.ds(PAD - offset + VIRTUAL * j + starts[k], WIDTH), :]
            kept = jnp.where(want == k, rows, kept)
            length = jnp.where(want == k, size_ref[k], length)
        out_ref[j] = jnp.where(t < length, kept, 0.0).astype(BF16)


def pack_amplitudes(place_ref, size_ref, occ_ref, a_ref, out_ref, pick_ref, main_ref, rest_ref, line_ref):
    xl, z, co, xh, y = [place_ref[i] for i in range(5)]
    starts = block_starts(size_ref)
    first = (xl * 32 + z * 2 + co) * 16 + (xh * 4 + y) * 2
    d = lax.broadcasted_iota(jnp.int32, (VIRTUAL, 2 * MAIN), 0)
    lane = lax.broadcasted_iota(jnp.int32, (VIRTUAL, 2 * MAIN), 1)
    t = jnp.where(lane < MAIN, lane, MAIN + lane % REST)
    for k in range(4):
        pick_ref[:, 2 * MAIN * k : 2 * MAIN * (k + 1)] = jnp.where(
            d == t + starts[k], 1.0, 0.0
        ).astype(BF16)
    row = lax.broadcasted_iota(jnp.int32, (8 * PITCH, 1), 0)
    orbital = block_of(starts, row % PITCH * 8 + row // PITCH)
    group = lax.broadcasted_iota(jnp.int32, (16, MAIN), 1) // REST
    for i in range(2):
        pair = first + i
        label = jnp.bitwise_xor(occ_ref[pair // OCCUPIED], occ_ref[pair % OCCUPIED])
        want = jnp.bitwise_xor(orbital, label)
        for e in range(8):
            line_ref[e * PITCH : e * PITCH + 50] = a_ref[i, :, VIRTUAL * e : VIRTUAL * (e + 1)]
        picked = jnp.dot(line_ref[...], pick_ref[...], preferred_element_type=F32)
        kept = jnp.zeros((8 * PITCH, 2 * MAIN), F32)
        for k in range(4):
            kept = jnp.where(want == k, picked[:, 2 * MAIN * k : 2 * MAIN * (k + 1)], kept)
        for e in range(8):
            main_ref[pl.ds(e, 50, stride=8)] = kept[e * PITCH : e * PITCH + 50, :MAIN]
            rest_ref[pl.ds(e, 50, stride=8)] = kept[e * PITCH : e * PITCH + 50, MAIN:]
        for v in range(GROUPS):
            packed = jnp.zeros((16, MAIN), F32)
            for m in range(4):
                w = 4 * v + m
                if w >= TILES:
                    continue
                c = w // WINDOWS * 200 + w % WINDOWS
                places = [pl.ds(c + 12 * h + 25 * u, 4, stride=25) for h in range(2) for u in (4, 0)]
                mains = [main_ref[rows] for rows in places]
                rests = [rest_ref[rows] for rows in places]
                out_ref[i, :, MAIN * w : MAIN * (w + 1)] = jnp.concatenate(mains, 0).astype(BF16)
                packed = jnp.where(group == m, jnp.concatenate(rests, 0), packed)
            lo = MAIN * (TILES + v)
            out_ref[i, :, lo : lo + MAIN] = packed.astype(BF16)


def multiply(place_ref, size_ref, label_ref, a_ref, b00_ref, b01_ref, b10_ref, b11_ref, out_ref, b_ref, sum_ref):
    xl, z, co, xh, y = [place_ref[i] for i in range(5)]
    starts = block_starts(size_ref)
    low = TILES * MAIN
    spare = DEPTH - low - TILES * REST
    b_ref[low + TILES * REST :] = jnp.zeros((spare, 256), BF16)
    for w in (0, 6, 12, 13, 19, 25):
        b_ref[w * MAIN : (w + 1) * MAIN] = jnp.zeros((MAIN, 256), BF16)
        b_ref[low + w * REST : low + (w + 1) * REST] = jnp.zeros((REST, 256), BF16)
    for flip_co, refs in ((0, (b00_ref, b10_ref)), (1, (b01_ref, b11_ref))):
        for flip_xl, from_ref in enumerate(refs):
            base = jnp.bitwise_xor(xl, flip_xl) * WINDOWS + jnp.bitwise_xor(co, flip_co) * 6
            for flip_xh in range(2):
                lanes = slice(flip_xh * 128, (flip_xh + 1) * 128)
                for j in range(SEGMENTS):
                    upper = pl.ds(pl.multiple_of((base + j) * MAIN, MAIN), MAIN)
                    lower = pl.ds(pl.multiple_of(low + (base + j) * REST, REST), REST)
                    head = from_ref[flip_xh, j, 0:MAIN]
                    tail = from_ref[flip_xh, j, MAIN:WIDTH]
                    if j in (0, 6):
                        head = head + b_ref[upper, lanes]
                        tail = tail + b_ref[lower, lanes]
                    b_ref[upper, lanes] = head
                    b_ref[lower, lanes] = tail
    total = jnp.dot(a_ref[...], b_ref[...], preferred_element_type=F32)
    for flip_xh in range(2):
        there = jnp.bitwise_xor(xh, flip_xh)
        label = column_label(starts, (there * 4 + y) * 128)
        part = jnp.where(
            label_ref[...] == label, total[:, flip_xh * 128 : (flip_xh + 1) * 128], 0.0
        )
        sum_ref[...] = part
        for yy in range(4):
            for zz in range(16):
                out_ref[(zz + 8) % 16, there, 2 * yy : 2 * yy + 2] = sum_ref[
                    32 * yy + 2 * zz : 32 * yy + 2 * zz + 2
                ]


def in_vmem(count):
    return [pl.BlockSpec(memory_space=pltpu.VMEM)] * count


def in_smem(count):
    return [pl.BlockSpec(memory_space=pltpu.SMEM)] * count


def call(kernel, out_shape, out_type, specs, scratch):
    return pl.pallas_call(
        kernel,
        out_shape=jax.ShapeDtypeStruct(out_shape, out_type),
        in_specs=specs,
        out_specs=pl.BlockSpec(memory_space=pltpu.VMEM),
        scratch_shapes=scratch,
        compiler_params=pltpu.CompilerParams(vmem_limit_bytes=40 * 1024 * 1024),
    )


def run_pack_integrals(place, block_sizes, integrals):
    return call(
        pack_integrals,
        (SEGMENTS, WIDTH, 128),
        BF16,
        in_smem(2) + in_vmem(1),
        [pltpu.VMEM((PAD + SEGMENTS * VIRTUAL + WIDTH, 128), F32)],
    )(place, block_sizes, integrals)


def run_pack_amplitudes(place, block_sizes, occ_irreps, amplitudes):
    return call(
        pack_amplitudes,
        (2, 16, DEPTH),
        BF16,
        in_smem(3) + in_vmem(1),
        [
            pltpu.VMEM((VIRTUAL, 8 * MAIN), BF16),
            pltpu.VMEM((VIRTUAL, MAIN), F32),
            pltpu.VMEM((VIRTUAL, MAIN), F32),
            pltpu.VMEM((8 * PITCH, VIRTUAL), BF16),
        ],
    )(place, block_sizes, occ_irreps, amplitudes.reshape(2, 50, 8 * VIRTUAL))


def run_multiply(place, block_sizes, labels, spread, blocks):
    return call(
        multiply,
        (16, 2, 8, 128),
        F32,
        in_smem(2) + in_vmem(6),
        [pltpu.VMEM((DEPTH, 256), BF16), pltpu.VMEM((128, 128), F32)],
    )(place, block_sizes, labels, spread, *blocks)


def row_labels(place, occ_irreps):
    row = jnp.arange(128, dtype=jnp.int32)
    xl, z, co, xh, y = [place[i] for i in range(5)]
    pair = xl * 512 + ((row // 2 + 8) % 16) * 32 + co * 16 + xh * 8 + (row // 32) * 2 + row % 2
    orbitals = jnp.arange(OCCUPIED, dtype=jnp.int32)[None, :]
    irreps = occ_irreps[None, :]
    one = jnp.sum(jnp.where((pair // OCCUPIED)[:, None] == orbitals, irreps, 0), axis=1)
    two = jnp.sum(jnp.where((pair % OCCUPIED)[:, None] == orbitals, irreps, 0), axis=1)
    return jnp.bitwise_xor(one, two)[:, None]


def swap(array, axis):
    return lax.ppermute(array, axis, [(0, 1), (1, 0)])


def on_device(amplitudes, integrals, occ_irreps, block_sizes):
    place = jnp.stack([lax.axis_index(n) for n in ("xl", "z", "co", "xh", "y")]).astype(jnp.int32)
    packed_a = run_pack_amplitudes(place, block_sizes, occ_irreps, amplitudes)
    sent = packed_a.reshape(2, 2, 8, DEPTH).transpose(2, 1, 0, 3).reshape(16, 2, DEPTH)
    sent, integrals = lax.optimization_barrier((sent, integrals))
    came = lax.all_to_all(
        sent, "z", split_axis=0, concat_axis=0, tiled=True, axis_index_groups=[[(i + 8) % 16 for i in range(16)]]
    )
    packed_b = run_pack_integrals(place, block_sizes, integrals)
    pair_b = jnp.stack([packed_b, swap(packed_b, "xh")])
    far_b = swap(pair_b, "xl")
    copies = jnp.broadcast_to(came.reshape(1, 32, DEPTH), (4, 32, DEPTH))
    spread = lax.all_to_all(copies, "y", split_axis=0, concat_axis=0, tiled=True)
    blocks_b = [pair_b, swap(pair_b, "co"), far_b, swap(far_b, "co")]
    labels = row_labels(place, occ_irreps)
    parts = run_multiply(place, block_sizes, labels, spread.reshape(128, DEPTH), blocks_b)
    pieces = lax.all_to_all(
        parts.reshape(32, 8, 128), ("z", "xh"), split_axis=0, concat_axis=0, tiled=True
    )
    total = jnp.sum(pieces.reshape(16, 2, 8, 128), axis=0)
    return total.reshape(16, 128).astype(BF16)


def solution(mesh):
    split = Mesh(mesh.devices.reshape(2, 16, 2, 2, 4), ("xl", "z", "co", "xh", "y"))
    row, col = ("xl", "z", "co"), ("xh", "y")
    return jax.shard_map(
        on_device,
        mesh=split,
        in_specs=(P(row + col, None), P(row, col), P(), P()),
        out_specs=P(row, col),
        check_vma=False,
    )
```

```python
import jax
import jax.numpy as jnp
from jax import lax
from jax.experimental import pallas as pl
from jax.experimental.pallas import tpu as pltpu
from jax.sharding import Mesh, PartitionSpec as P

OCCUPIED = 50
VIRTUAL = 400
WIDTH = 160
RANGE = 2500
SEGMENTS = 7
WINDOWS = 13
MAIN = 128
REST = WIDTH - MAIN
TILES = 2 * WINDOWS
GROUPS = -(-TILES // 4)
DEPTH = (TILES + GROUPS) * MAIN
PAD = 304
PITCH = 64
HEAD = SEGMENTS * MAIN
BF16 = jnp.bfloat16
F32 = jnp.float32


def block_starts(size_ref):
    starts = [0]
    for k in range(3):
        starts.append(starts[-1] + size_ref[k])
    return starts


def block_of(starts, value):
    label = jnp.where(value >= starts[1], 1, 0)
    label = label + jnp.where(value >= starts[2], 1, 0)
    return label + jnp.where(value >= starts[3], 1, 0)


def column_label(starts, first):
    s = first + lax.broadcasted_iota(jnp.int32, (1, 128), 1)
    a = jnp.where(s >= VIRTUAL, 1, 0) + jnp.where(s >= 2 * VIRTUAL, 1, 0)
    return jnp.bitwise_xor(block_of(starts, a), block_of(starts, s - VIRTUAL * a))


def pack_integrals(place_ref, size_ref, b_ref, out_ref, pad_ref):
    xl, z, co, xh, y = [place_ref[i] for i in range(5)]
    starts = block_starts(size_ref)
    first = RANGE * (xl * 32 + z * 2 + co)
    orbital = first // VIRTUAL
    offset = first - orbital * VIRTUAL
    label = column_label(starts, (xh * 4 + y) * 128)
    after = pad_ref.shape[0] - PAD - RANGE
    pad_ref[0:PAD] = jnp.zeros((PAD, 128), F32)
    pad_ref[PAD + RANGE :] = jnp.zeros((after, 128), F32)
    pad_ref[PAD : PAD + RANGE] = b_ref[...].astype(F32)
    t = lax.broadcasted_iota(jnp.int32, (WIDTH, 128), 0)
    for j in range(SEGMENTS):
        want = jnp.bitwise_xor(block_of(starts, orbital + j), label)
        kept = jnp.zeros((WIDTH, 128), F32)
        length = jnp.zeros((1, 128), jnp.int32)
        for k in range(4):
            rows = pad_ref[pl.ds(PAD - offset + VIRTUAL * j + starts[k], WIDTH), :]
            kept = jnp.where(want == k, rows, kept)
            length = jnp.where(want == k, size_ref[k], length)
        kept = jnp.where(t < length, kept, 0.0).astype(BF16)
        out_ref[MAIN * j : MAIN * (j + 1)] = kept[:MAIN]
        out_ref[HEAD + REST * j : HEAD + REST * (j + 1)] = kept[MAIN:]


def pack_amplitudes(place_ref, size_ref, occ_ref, a_ref, out_ref, pick_ref, main_ref, rest_ref, line_ref):
    xl, z, co, xh, y = [place_ref[i] for i in range(5)]
    starts = block_starts(size_ref)
    first = (xl * 32 + z * 2 + co) * 16 + (xh * 4 + y) * 2
    d = lax.broadcasted_iota(jnp.int32, (VIRTUAL, 2 * MAIN), 0)
    lane = lax.broadcasted_iota(jnp.int32, (VIRTUAL, 2 * MAIN), 1)
    t = jnp.where(lane < MAIN, lane, MAIN + lane % REST)
    for k in range(4):
        pick_ref[:, 2 * MAIN * k : 2 * MAIN * (k + 1)] = jnp.where(
            d == t + starts[k], 1.0, 0.0
        ).astype(BF16)
    row = lax.broadcasted_iota(jnp.int32, (8 * PITCH, 1), 0)
    orbital = block_of(starts, row % PITCH * 8 + row // PITCH)
    group = lax.broadcasted_iota(jnp.int32, (16, MAIN), 1) // REST
    for i in range(2):
        pair = first + i
        label = jnp.bitwise_xor(occ_ref[pair // OCCUPIED], occ_ref[pair % OCCUPIED])
        want = jnp.bitwise_xor(orbital, label)
        for e in range(8):
            line_ref[e * PITCH : e * PITCH + 50] = a_ref[i, :, VIRTUAL * e : VIRTUAL * (e + 1)]
        picked = jnp.dot(line_ref[...], pick_ref[...], preferred_element_type=F32)
        kept = jnp.zeros((8 * PITCH, 2 * MAIN), F32)
        for k in range(4):
            kept = jnp.where(want == k, picked[:, 2 * MAIN * k : 2 * MAIN * (k + 1)], kept)
        for e in range(8):
            main_ref[pl.ds(e, 50, stride=8)] = kept[e * PITCH : e * PITCH + 50, :MAIN]
            rest_ref[pl.ds(e, 50, stride=8)] = kept[e * PITCH : e * PITCH + 50, MAIN:]
        for v in range(GROUPS):
            packed = jnp.zeros((16, MAIN), F32)
            for m in range(4):
                w = 4 * v + m
                if w >= TILES:
                    continue
                c = w // WINDOWS * 200 + w % WINDOWS
                places = [pl.ds(c + 12 * h + 25 * u, 4, stride=25) for h in range(2) for u in (4, 0)]
                mains = [main_ref[rows] for rows in places]
                rests = [rest_ref[rows] for rows in places]
                out_ref[i, :, MAIN * w : MAIN * (w + 1)] = jnp.concatenate(mains, 0).astype(BF16)
                packed = jnp.where(group == m, jnp.concatenate(rests, 0), packed)
            lo = MAIN * (TILES + v)
            out_ref[i, :, lo : lo + MAIN] = packed.astype(BF16)


def multiply(place_ref, size_ref, label_ref, a_ref, b00_ref, b01_ref, b10_ref, b11_ref, out_ref, rest_ref, sum_ref):
    xl, z, co, xh, y = [place_ref[i] for i in range(5)]
    starts = block_starts(size_ref)
    low = TILES * MAIN
    rest_ref[TILES * REST :] = jnp.zeros((DEPTH - low - TILES * REST, 256), BF16)
    for w in (0, 6, 12, 13, 19, 25):
        rest_ref[w * REST : (w + 1) * REST] = jnp.zeros((REST, 256), BF16)
    totals = [jnp.zeros((128, 128), F32), jnp.zeros((128, 128), F32)]
    for flip_co, refs in ((0, (b00_ref, b10_ref)), (1, (b01_ref, b11_ref))):
        for flip_xl, from_ref in enumerate(refs):
            base = jnp.bitwise_xor(xl, flip_xl) * WINDOWS + jnp.bitwise_xor(co, flip_co) * 6
            left = a_ref[:, pl.ds(pl.multiple_of(base * MAIN, MAIN), HEAD)]
            for flip_xh in range(2):
                totals[flip_xh] += jnp.dot(
                    left, from_ref[flip_xh, 0:HEAD], preferred_element_type=F32
                )
                lanes = slice(flip_xh * 128, (flip_xh + 1) * 128)
                for j in range(SEGMENTS):
                    lower = pl.ds(pl.multiple_of((base + j) * REST, REST), REST)
                    tail = from_ref[flip_xh, HEAD + REST * j : HEAD + REST * (j + 1)]
                    if j in (0, 6):
                        tail = tail + rest_ref[lower, lanes]
                    rest_ref[lower, lanes] = tail
    total = jnp.concatenate(totals, 1) + jnp.dot(
        a_ref[:, low:], rest_ref[...], preferred_element_type=F32
    )
    for flip_xh in range(2):
        there = jnp.bitwise_xor(xh, flip_xh)
        label = column_label(starts, (there * 4 + y) * 128)
        part = jnp.where(
            label_ref[...] == label, total[:, flip_xh * 128 : (flip_xh + 1) * 128], 0.0
        )
        sum_ref[...] = part
        for yy in range(4):
            for zz in range(16):
                out_ref[(zz + 8) % 16, there, 2 * yy : 2 * yy + 2] = sum_ref[
                    32 * yy + 2 * zz : 32 * yy + 2 * zz + 2
                ]


def in_vmem(count):
    return [pl.BlockSpec(memory_space=pltpu.VMEM)] * count


def in_smem(count):
    return [pl.BlockSpec(memory_space=pltpu.SMEM)] * count


def call(kernel, out_shape, out_type, specs, scratch):
    return pl.pallas_call(
        kernel,
        out_shape=jax.ShapeDtypeStruct(out_shape, out_type),
        in_specs=specs,
        out_specs=pl.BlockSpec(memory_space=pltpu.VMEM),
        scratch_shapes=scratch,
        compiler_params=pltpu.CompilerParams(vmem_limit_bytes=40 * 1024 * 1024),
    )


def run_pack_integrals(place, block_sizes, integrals):
    return call(
        pack_integrals,
        (SEGMENTS * WIDTH, 128),
        BF16,
        in_smem(2) + in_vmem(1),
        [pltpu.VMEM((PAD + SEGMENTS * VIRTUAL + WIDTH, 128), F32)],
    )(place, block_sizes, integrals)


def run_pack_amplitudes(place, block_sizes, occ_irreps, amplitudes):
    return call(
        pack_amplitudes,
        (2, 16, DEPTH),
        BF16,
        in_smem(3) + in_vmem(1),
        [
            pltpu.VMEM((VIRTUAL, 8 * MAIN), BF16),
            pltpu.VMEM((VIRTUAL, MAIN), F32),
            pltpu.VMEM((VIRTUAL, MAIN), F32),
            pltpu.VMEM((8 * PITCH, VIRTUAL), BF16),
        ],
    )(place, block_sizes, occ_irreps, amplitudes.reshape(2, 50, 8 * VIRTUAL))


def run_multiply(place, block_sizes, labels, spread, blocks):
    return call(
        multiply,
        (16, 2, 8, 128),
        F32,
        in_smem(2) + in_vmem(6),
        [pltpu.VMEM((DEPTH - TILES * MAIN, 256), BF16), pltpu.VMEM((128, 128), F32)],
    )(place, block_sizes, labels, spread, *blocks)


def row_labels(place, occ_irreps):
    row = jnp.arange(128, dtype=jnp.int32)
    xl, z, co, xh, y = [place[i] for i in range(5)]
    pair = xl * 512 + ((row // 2 + 8) % 16) * 32 + co * 16 + xh * 8 + (row // 32) * 2 + row % 2
    orbitals = jnp.arange(OCCUPIED, dtype=jnp.int32)[None, :]
    irreps = occ_irreps[None, :]
    one = jnp.sum(jnp.where((pair // OCCUPIED)[:, None] == orbitals, irreps, 0), axis=1)
    two = jnp.sum(jnp.where((pair % OCCUPIED)[:, None] == orbitals, irreps, 0), axis=1)
    return jnp.bitwise_xor(one, two)[:, None]


def swap(array, axis):
    return lax.ppermute(array, axis, [(0, 1), (1, 0)])


def on_device(amplitudes, integrals, occ_irreps, block_sizes):
    place = jnp.stack([lax.axis_index(n) for n in ("xl", "z", "co", "xh", "y")]).astype(jnp.int32)
    packed_a = run_pack_amplitudes(place, block_sizes, occ_irreps, amplitudes)
    sent = packed_a.reshape(2, 2, 8, DEPTH).transpose(2, 1, 0, 3).reshape(16, 2, DEPTH)
    sent, integrals = lax.optimization_barrier((sent, integrals))
    came = lax.all_to_all(
        sent, "z", split_axis=0, concat_axis=0, tiled=True, axis_index_groups=[[(i + 8) % 16 for i in range(16)]]
    )
    packed_b = run_pack_integrals(place, block_sizes, integrals)
    pair_b = jnp.stack([packed_b, swap(packed_b, "xh")])
    far_b = swap(pair_b, "xl")
    copies = jnp.broadcast_to(came.reshape(1, 32, DEPTH), (4, 32, DEPTH))
    spread = lax.all_to_all(copies, "y", split_axis=0, concat_axis=0, tiled=True)
    blocks_b = [pair_b, swap(pair_b, "co"), far_b, swap(far_b, "co")]
    labels = row_labels(place, occ_irreps)
    parts = run_multiply(place, block_sizes, labels, spread.reshape(128, DEPTH), blocks_b)
    pieces = lax.all_to_all(
        parts.reshape(32, 8, 128), ("z", "xh"), split_axis=0, concat_axis=0, tiled=True
    )
    total = jnp.sum(pieces.reshape(16, 2, 8, 128), axis=0)
    return total.reshape(16, 128).astype(BF16)


def solution(mesh):
    split = Mesh(mesh.devices.reshape(2, 16, 2, 2, 4), ("xl", "z", "co", "xh", "y"))
    row, col = ("xl", "z", "co"), ("xh", "y")
    return jax.shard_map(
        on_device,
        mesh=split,
        in_specs=(P(row + col, None), P(row, col), P(), P()),
        out_specs=P(row, col),
        check_vma=False,
    )
```

```python
import jax
import jax.numpy as jnp
from jax import lax
from jax.experimental import pallas as pl
from jax.experimental.pallas import tpu as pltpu
from jax.sharding import Mesh, PartitionSpec as P

OCCUPIED = 50
VIRTUAL = 400
WIDTH = 160
RANGE = 2500
SEGMENTS = 7
WINDOWS = 13
MAIN = 128
REST = WIDTH - MAIN
TILES = 2 * WINDOWS
GROUPS = -(-TILES // 4)
DEPTH = (TILES + GROUPS) * MAIN
PAD = 304
PITCH = 64
HEAD = SEGMENTS * MAIN
BF16 = jnp.bfloat16
F32 = jnp.float32


def block_starts(size_ref):
    starts = [0]
    for k in range(3):
        starts.append(starts[-1] + size_ref[k])
    return starts


def block_of(starts, value):
    label = jnp.where(value >= starts[1], 1, 0)
    label = label + jnp.where(value >= starts[2], 1, 0)
    return label + jnp.where(value >= starts[3], 1, 0)


def column_label(starts, first):
    s = first + lax.broadcasted_iota(jnp.int32, (1, 128), 1)
    a = jnp.where(s >= VIRTUAL, 1, 0) + jnp.where(s >= 2 * VIRTUAL, 1, 0)
    return jnp.bitwise_xor(block_of(starts, a), block_of(starts, s - VIRTUAL * a))


def pack_integrals(place_ref, size_ref, b_ref, out_ref, pad_ref):
    xl, z, co, xh, y = [place_ref[i] for i in range(5)]
    starts = block_starts(size_ref)
    first = RANGE * (xl * 32 + z * 2 + co)
    orbital = first // VIRTUAL
    offset = first - orbital * VIRTUAL
    label = column_label(starts, (xh * 4 + y) * 128)
    after = pad_ref.shape[0] - PAD - RANGE
    pad_ref[0:PAD] = jnp.zeros((PAD, 128), F32)
    pad_ref[PAD + RANGE :] = jnp.zeros((after, 128), F32)
    pad_ref[PAD : PAD + RANGE] = b_ref[...].astype(F32)
    t = lax.broadcasted_iota(jnp.int32, (WIDTH, 128), 0)
    for j in range(SEGMENTS):
        want = jnp.bitwise_xor(block_of(starts, orbital + j), label)
        kept = jnp.zeros((WIDTH, 128), F32)
        length = jnp.zeros((1, 128), jnp.int32)
        for k in range(4):
            rows = pad_ref[pl.ds(PAD - offset + VIRTUAL * j + starts[k], WIDTH), :]
            kept = jnp.where(want == k, rows, kept)
            length = jnp.where(want == k, size_ref[k], length)
        kept = jnp.where(t < length, kept, 0.0).astype(BF16)
        out_ref[MAIN * j : MAIN * (j + 1)] = kept[:MAIN]
        out_ref[HEAD + REST * j : HEAD + REST * (j + 1)] = kept[MAIN:]


def pack_amplitudes(place_ref, size_ref, occ_ref, a_ref, out_ref, pick_ref, main_ref, rest_ref, line_ref):
    xl, z, co, xh, y = [place_ref[i] for i in range(5)]
    starts = block_starts(size_ref)
    first = (xl * 32 + z * 2 + co) * 16 + (xh * 4 + y) * 2
    d = lax.broadcasted_iota(jnp.int32, (VIRTUAL, 2 * MAIN), 0)
    lane = lax.broadcasted_iota(jnp.int32, (VIRTUAL, 2 * MAIN), 1)
    t = jnp.where(lane < MAIN, lane, MAIN + lane % REST)
    for k in range(4):
        pick_ref[:, 2 * MAIN * k : 2 * MAIN * (k + 1)] = jnp.where(
            d == t + starts[k], 1.0, 0.0
        ).astype(BF16)
    row = lax.broadcasted_iota(jnp.int32, (8 * PITCH, 1), 0)
    orbital = block_of(starts, row % PITCH * 8 + row // PITCH)
    group = lax.broadcasted_iota(jnp.int32, (16, MAIN), 1) // REST
    for i in range(2):
        pair = first + i
        label = jnp.bitwise_xor(occ_ref[pair // OCCUPIED], occ_ref[pair % OCCUPIED])
        want = jnp.bitwise_xor(orbital, label)
        for e in range(8):
            line_ref[e * PITCH : e * PITCH + 50] = a_ref[i, :, VIRTUAL * e : VIRTUAL * (e + 1)]
        picked = jnp.dot(line_ref[...], pick_ref[...], preferred_element_type=F32)
        kept = jnp.zeros((8 * PITCH, 2 * MAIN), F32)
        for k in range(4):
            kept = jnp.where(want == k, picked[:, 2 * MAIN * k : 2 * MAIN * (k + 1)], kept)
        for e in range(8):
            main_ref[pl.ds(e, 50, stride=8)] = kept[e * PITCH : e * PITCH + 50, :MAIN]
            rest_ref[pl.ds(e, 50, stride=8)] = kept[e * PITCH : e * PITCH + 50, MAIN:]
        for v in range(GROUPS):
            packed = jnp.zeros((16, MAIN), F32)
            for m in range(4):
                w = 4 * v + m
                if w >= TILES:
                    continue
                c = w // WINDOWS * 200 + w % WINDOWS
                places = [pl.ds(c + 12 * h + 25 * u, 4, stride=25) for h in range(2) for u in (4, 0)]
                mains = [main_ref[rows] for rows in places]
                rests = [rest_ref[rows] for rows in places]
                out_ref[i, :, MAIN * w : MAIN * (w + 1)] = jnp.concatenate(mains, 0).astype(BF16)
                packed = jnp.where(group == m, jnp.concatenate(rests, 0), packed)
            lo = MAIN * (TILES + v)
            out_ref[i, :, lo : lo + MAIN] = packed.astype(BF16)


def multiply(place_ref, size_ref, label_ref, a_ref, b00_ref, b01_ref, b10_ref, b11_ref, out_ref, rest_ref, sum_ref):
    xl, z, co, xh, y = [place_ref[i] for i in range(5)]
    starts = block_starts(size_ref)
    low = TILES * MAIN
    rest_ref[TILES * REST :] = jnp.zeros((DEPTH - low - TILES * REST, 256), BF16)
    for w in (0, 6, 12, 13, 19, 25):
        rest_ref[w * REST : (w + 1) * REST] = jnp.zeros((REST, 256), BF16)
    totals = [jnp.zeros((128, 128), F32), jnp.zeros((128, 128), F32)]
    for flip_co, refs in ((0, (b00_ref, b10_ref)), (1, (b01_ref, b11_ref))):
        for flip_xl, from_ref in enumerate(refs):
            base = jnp.bitwise_xor(xl, flip_xl) * WINDOWS + jnp.bitwise_xor(co, flip_co) * 6
            left = a_ref[:, pl.ds(pl.multiple_of(base * MAIN, MAIN), HEAD)]
            for flip_xh in range(2):
                totals[flip_xh] += jnp.dot(
                    left, from_ref[flip_xh, 0:HEAD], preferred_element_type=F32
                )
                lanes = slice(flip_xh * 128, (flip_xh + 1) * 128)
                for j in range(SEGMENTS):
                    lower = pl.ds(pl.multiple_of((base + j) * REST, REST), REST)
                    tail = from_ref[flip_xh, HEAD + REST * j : HEAD + REST * (j + 1)]
                    if j in (0, 6):
                        tail = tail + rest_ref[lower, lanes]
                    rest_ref[lower, lanes] = tail
    total = jnp.concatenate(totals, 1) + jnp.dot(
        a_ref[:, low:], rest_ref[...], preferred_element_type=F32
    )
    for flip_xh in range(2):
        there = jnp.bitwise_xor(xh, flip_xh)
        label = column_label(starts, (there * 4 + y) * 128)
        part = jnp.where(
            label_ref[...] == label, total[:, flip_xh * 128 : (flip_xh + 1) * 128], 0.0
        )
        sum_ref[0:128] = part
        for zz in range(16):
            pieces = [sum_ref[32 * yy + 2 * zz : 32 * yy + 2 * zz + 2] for yy in range(4)]
            out_ref[(zz + 8) % 16, there] = jnp.concatenate(pieces, 0)


def in_vmem(count):
    return [pl.BlockSpec(memory_space=pltpu.VMEM)] * count


def in_smem(count):
    return [pl.BlockSpec(memory_space=pltpu.SMEM)] * count


def call(kernel, out_shape, out_type, specs, scratch):
    return pl.pallas_call(
        kernel,
        out_shape=jax.ShapeDtypeStruct(out_shape, out_type),
        in_specs=specs,
        out_specs=pl.BlockSpec(memory_space=pltpu.VMEM),
        scratch_shapes=scratch,
        compiler_params=pltpu.CompilerParams(vmem_limit_bytes=40 * 1024 * 1024),
    )


def run_pack_integrals(place, block_sizes, integrals):
    return call(
        pack_integrals,
        (SEGMENTS * WIDTH, 128),
        BF16,
        in_smem(2) + in_vmem(1),
        [pltpu.VMEM((PAD + SEGMENTS * VIRTUAL + WIDTH, 128), F32)],
    )(place, block_sizes, integrals)


def run_pack_amplitudes(place, block_sizes, occ_irreps, amplitudes):
    return call(
        pack_amplitudes,
        (2, 16, DEPTH),
        BF16,
        in_smem(3) + in_vmem(1),
        [
            pltpu.VMEM((VIRTUAL, 8 * MAIN), BF16),
            pltpu.VMEM((512, MAIN), F32),
            pltpu.VMEM((512, MAIN), F32),
            pltpu.VMEM((8 * PITCH, VIRTUAL), BF16),
        ],
    )(place, block_sizes, occ_irreps, amplitudes.reshape(2, 50, 8 * VIRTUAL))


def run_multiply(place, block_sizes, labels, spread, blocks):
    return call(
        multiply,
        (16, 2, 8, 128),
        F32,
        in_smem(2) + in_vmem(6),
        [pltpu.VMEM((DEPTH - TILES * MAIN, 256), BF16), pltpu.VMEM((136, 128), F32)],
    )(place, block_sizes, labels, spread, *blocks)


def row_labels(place, occ_irreps):
    row = jnp.arange(128, dtype=jnp.int32)
    xl, z, co, xh, y = [place[i] for i in range(5)]
    pair = xl * 512 + ((row // 2 + 8) % 16) * 32 + co * 16 + xh * 8 + (row // 32) * 2 + row % 2
    orbitals = jnp.arange(OCCUPIED, dtype=jnp.int32)[None, :]
    irreps = occ_irreps[None, :]
    one = jnp.sum(jnp.where((pair // OCCUPIED)[:, None] == orbitals, irreps, 0), axis=1)
    two = jnp.sum(jnp.where((pair % OCCUPIED)[:, None] == orbitals, irreps, 0), axis=1)
    return jnp.bitwise_xor(one, two)[:, None]


def swap(array, axis):
    return lax.ppermute(array, axis, [(0, 1), (1, 0)])


def on_device(amplitudes, integrals, occ_irreps, block_sizes):
    place = jnp.stack([lax.axis_index(n) for n in ("xl", "z", "co", "xh", "y")]).astype(jnp.int32)
    packed_a = run_pack_amplitudes(place, block_sizes, occ_irreps, amplitudes)
    sent = packed_a.reshape(2, 2, 8, DEPTH).transpose(2, 1, 0, 3).reshape(16, 2, DEPTH)
    sent, integrals = lax.optimization_barrier((sent, integrals))
    came = lax.all_to_all(
        sent, "z", split_axis=0, concat_axis=0, tiled=True, axis_index_groups=[[(i + 8) % 16 for i in range(16)]]
    )
    packed_b = run_pack_integrals(place, block_sizes, integrals)
    pair_b = jnp.stack([packed_b, swap(packed_b, "xh")])
    far_b = swap(pair_b, "xl")
    copies = jnp.broadcast_to(came.reshape(1, 32, DEPTH), (4, 32, DEPTH))
    spread = lax.all_to_all(copies, "y", split_axis=0, concat_axis=0, tiled=True)
    blocks_b = [pair_b, swap(pair_b, "co"), far_b, swap(far_b, "co")]
    labels = row_labels(place, occ_irreps)
    parts = run_multiply(place, block_sizes, labels, spread.reshape(128, DEPTH), blocks_b)
    pieces = lax.all_to_all(
        parts.reshape(32, 8, 128), ("z", "xh"), split_axis=0, concat_axis=0, tiled=True
    )
    total = jnp.sum(pieces.reshape(16, 2, 8, 128), axis=0)
    return total.reshape(16, 128).astype(BF16)


def solution(mesh):
    split = Mesh(mesh.devices.reshape(2, 16, 2, 2, 4), ("xl", "z", "co", "xh", "y"))
    row, col = ("xl", "z", "co"), ("xh", "y")
    return jax.shard_map(
        on_device,
        mesh=split,
        in_specs=(P(row + col, None), P(row, col), P(), P()),
        out_specs=P(row, col),
        check_vma=False,
    )
```
